32 devices in a mesh: panel: 8 (over y, x, core), row: 4 (over z).
Axes of the slice: x: 2, y: 2, z: 4, core: 2. Of those that a mesh axis runs over, the one named last changes fastest.
Arguments:
- slab: float32 [4096, 2048], P('row', 'panel'), may hold values from -6 to 6
- boundary: float32 [4096, 256], P('row'), may hold values from -6 to 6
- diag_inverse: float32 [2048, 256], P(('panel', 'row')), may hold values from -1 to 1.6, as said below
- sub_block: float32 [2048, 256], P(('panel', 'row')), may hold values from -0.375 to 0.375
- tail_coupling: float32 [2048, 256], P(('panel', 'row')), may hold values from -0.125 to 0.125
- tail_cols: float32 [4096, 256], P(('row', 'panel')), may hold values from -6 to 6
Outputs:
- factor: float32 [4096, 2048], P('row', 'panel')
- tail_out: float32 [4096, 256], P(('row', 'panel'))
The draws below stay inside these ranges and needn't reach their ends.
Inputs may be any that keep to these rules, and one draw needn't show every extreme that they name: `diag_inverse`: each block of 256 rows is lower triangular with a positive diagonal of 0.6 to 1.6.
All inputs are finite; a program needn't handle non-finite values.
Results may differ from the reference program's by a relative error of at most 0.00029.
Values sent between devices are 32-bit elements; how exact they have to be, the bound alone decides.
No kernel may reach another device: no remote copies, remote signals or barrier semaphores. Data moves between devices by JAX's collectives and lax.ppermute only.
A program may use at most 128 MiB of HBM per device.

```python
import math
import jax
import jax.numpy as jnp
from jax import lax

B = 256
PANELS = 8
ROWS = 4096


def draw_diag_inverse(key, part):
    key_diag, key_off = jax.random.split(jax.random.fold_in(key, 17))
    total = PANELS * B
    within = (jnp.arange(total) % B)[:, None]
    column = jnp.arange(B)[None, :]
    diagonal = jnp.exp(jax.random.uniform(key_diag, (total, 1), jnp.float32, math.log(0.7), math.log(1.4)))
    offdiag = jnp.clip(jax.random.normal(key_off, (total, B), jnp.float32), -4.0, 4.0) * (0.3 / math.sqrt(B))
    return jnp.where(column == within, diagonal, jnp.where(column < within, offdiag, 0.0)).astype(jnp.float32)


def shard_levels(own_key, dims, shards, smallest, high):
    def one(axis_at, shards_of):
        heights = jax.random.uniform(jax.random.fold_in(jax.random.fold_in(own_key, 6), axis_at), (shards_of,), jnp.float32, smallest / len(shards), high / len(shards))
        return jnp.repeat(jnp.exp(heights), dims[axis_at] // shards_of).reshape((-1,) + (1,) * (len(dims) - axis_at - 1))

    level = one(*shards[0])
    for cut in shards[1:]:
        level = level * one(*cut)
    return level


def centred(own_key, extent, deviation, most, cuts=(), dtype=jnp.bfloat16):
    entries = jax.random.normal(own_key, extent, jnp.float32) * deviation
    if len(cuts) > 0:
        entries = shard_levels(own_key, extent, cuts, -0.22, 0.18) * entries
    return jnp.clip(entries, min=-most, max=most).astype(dtype)


def setup_inputs(seed: int = 0) -> dict:
    streams_of = jax.random.split(jax.random.key(seed), 7)
    slab = centred(streams_of[0], (ROWS, PANELS * B), 1.0, 6.0, ((0, 4), (1, 8)), jnp.float32)
    boundary = centred(streams_of[1], (ROWS, B), 1.0, 6.0, ((0, 4),), jnp.float32)
    diag_inverse = draw_diag_inverse(jax.random.fold_in(streams_of[6], 71), 0)
    sub_block = centred(streams_of[3], (PANELS * B, B), (B + B // 10) ** -0.5, 0.375, ((0, 32),), jnp.float32)
    tail_coupling = centred(streams_of[4], (PANELS * B, B), (B * PANELS) ** -0.5, 0.125, ((0, 32),), jnp.float32)
    tail_cols = centred(streams_of[5], (ROWS, B), 1.0, 6.0, ((0, 32),), jnp.float32)
    return {"slab": slab, "boundary": boundary, "diag_inverse": diag_inverse, "sub_block": sub_block, "tail_coupling": tail_coupling, "tail_cols": tail_cols}


def transpose_dot(left, right):
    return lax.dot_general(left, right, (((1,), (1,)), ((), ())), precision=lax.Precision.HIGHEST, preferred_element_type=jnp.float32)


def reference(slab, boundary, diag_inverse, sub_block, tail_coupling, tail_cols):
    previous = boundary
    pieces = []
    summed = jnp.zeros((slab.shape[0], B), jnp.float32)
    for panel_index in range(PANELS):
        low = panel_index * B
        inverse = diag_inverse[low:low + B]
        beneath = sub_block[low:low + B]
        coupling = tail_coupling[low:low + B]
        solved = transpose_dot(slab[:, low:low + B] - transpose_dot(previous, beneath), inverse)
        summed = summed + jnp.dot(solved, coupling, precision=lax.Precision.HIGHEST, preferred_element_type=jnp.float32)
        pieces.append(solved)
        previous = solved
    return jnp.concatenate(pieces, axis=1), tail_cols - summed
```

```python
import functools

import jax
import jax.numpy as jnp
from jax import lax
from jax.experimental import pallas as pl
from jax.experimental.pallas import tpu as pltpu
from jax.sharding import PartitionSpec as P

CHUNKS = 2
NT = (((1,), (1,)), ((), ()))
NN = (((1,), (0,)), ((), ()))
VMEM = pl.BlockSpec(memory_space=pltpu.VMEM)


def split(x):
    high = x.astype(jnp.bfloat16)
    return high, (x - high.astype(jnp.float32)).astype(jnp.bfloat16)


def dot3(left, right, dims):
    dot = functools.partial(lax.dot_general, dimension_numbers=dims, preferred_element_type=jnp.float32)
    return dot(left[0], right[0]) + (dot(left[0], right[1]) + dot(left[1], right[0]))


def chip_and_core():
    panel = lax.axis_index("panel")
    return lax.div(panel, 2), lax.rem(panel, 2)


def call(kernel, outs, args, scratch=(), products=0):
    size = sum(a.size * 4 for a in args) + sum(o[0] * o[1] * 4 for o in outs)
    return pl.pallas_call(
        kernel,
        out_shape=[jax.ShapeDtypeStruct(o, jnp.float32) for o in outs],
        in_specs=[VMEM] * len(args),
        out_specs=[VMEM] * len(outs),
        scratch_shapes=list(scratch),
        compiler_params=pltpu.CompilerParams(vmem_limit_bytes=40 << 20),
        cost_estimate=pl.CostEstimate(flops=6 * products, bytes_accessed=size, transcendentals=0),
    )(*args)


def shard_rows(count, shift, height):
    start = lax.rem(lax.axis_index("row") + count - shift, count) * height
    return pl.ds(pl.multiple_of(start, height), height)


def take(refs, count):
    return [next(refs) for _ in range(count)]


def prepare(count, chunks, *refs):
    refs = iter(refs)
    own, other = take(refs, count), take(refs, count)
    keep, got, bound, coupling = take(refs, 4)
    part_ref, map_ref, both_ref, coupling_out = take(refs, 4)
    carry_refs = take(refs, chunks)
    inverse, beneath = take(refs, 2)
    chip, core = chip_and_core()
    coupling_out[...] = coupling[...]
    height = own[0].shape[0] // 2
    for shift in range(count):
        rows = shard_rows(count, shift, height)
        for slot, shards in ((core, own), (1 - core, other)):
            inverse[slot, rows, :] = shards[shift][:height, :]
            beneath[slot, rows, :] = shards[shift][height:, :]
    inverse_a, inverse_b = split(inverse[0]), split(inverse[1])
    map_a = dot3(inverse_a, split(beneath[0]), NN)
    map_b = dot3(inverse_b, split(beneath[1]), NN)
    parts_a, parts_b = split(map_a), split(map_b)
    map_ref[...] = map_a
    both_ref[...] = dot3(parts_b, parts_a, NN)
    first = core == 0
    part_ref[...] = dot3(split(jnp.where(first, keep[...], got[...])), inverse_a, NT)

    @pl.when(chip == 0)
    def _():
        part_ref[...] -= dot3(split(bound[...]), parts_a, NT)

    carry = dot3(split(jnp.where(first, got[...], keep[...])), inverse_b, NT)
    carry -= dot3(split(part_ref[...]), parts_b, NT)
    height = carry.shape[0] // chunks
    for k in range(chunks):
        carry_refs[k][...] = carry[k * height : (k + 1) * height]


def inclusive(carry, prior, both, out):
    out[...] = carry[...] + dot3(split(prior[...]), split(both[...]), NT)


def absorb(half, prior, across, arrived, put):
    total = arrived[0][...]
    for more in arrived[1:]:
        total = total + more[...]
    chip, _ = chip_and_core()
    inner = lax.rem(chip, half) != 0

    @pl.when(inner)
    def _():
        put(prior[...] + dot3(split(total), split(across[...]), NT))

    @pl.when(jnp.logical_not(inner))
    def _():
        put(prior[...] + total)


def advance(half, prior, across, *refs):
    *arrived, out = refs

    def put(value):
        out[...] = value

    absorb(half, prior, across, arrived, put)


def extend(half, across, arrived, out):
    chip, _ = chip_and_core()
    inner = lax.rem(chip, half) != 0
    upper = lax.rem(chip, 2 * half) >= half
    out[...] = across[...]

    @pl.when(jnp.logical_and(upper, inner))
    def _():
        out[...] = dot3(split(across[...]), split(arrived[...]), NN)

    @pl.when(jnp.logical_and(upper, jnp.logical_not(inner)))
    def _():
        out[...] = arrived[...]


def joined(half, both, across, out):
    chip, _ = chip_and_core()
    out[...] = both[...]

    @pl.when(lax.rem(chip, half) != 0)
    def _():
        out[...] = dot3(split(both[...]), split(across[...]), NN)


def finish(count, chunks, half, arrivals, *refs):
    refs = iter(refs)
    part, map_ref, both = take(refs, 3)
    across = next(refs) if arrivals else None
    carries, priors = take(refs, chunks), take(refs, chunks)
    arrived = [take(refs, arrivals) for _ in range(chunks)]
    own, other = take(refs, count), take(refs, count)
    stay, leave, tail, coupling, entering = take(refs, 5)
    _, core = chip_and_core()
    height = own[0].shape[0]
    for shift in range(count):
        rows = shard_rows(count, shift, height)
        coupling[core, rows, :] = own[shift][...]
        coupling[1 - core, rows, :] = other[shift][...]
    map_a, map_ab = split(map_ref[...]), split(both[...])
    coupling_a, coupling_b = split(coupling[0]), split(coupling[1])
    first = core == 0
    height = carries[0].shape[0]
    for k in range(chunks):
        rows = slice(k * height, (k + 1) * height)

        def put(value, rows=rows):
            entering[rows, :] = value

        if arrivals:
            absorb(half, priors[k], across, arrived[k], put)
        else:
            put(priors[k][...])
        incoming = split(entering[rows, :])
        solved_a = part[rows, :] - dot3(incoming, map_a, NT)
        solved_b = carries[k][...] + dot3(incoming, map_ab, NT)
        stay[rows, :] = jnp.where(first, solved_a, solved_b)
        leave[rows, :] = jnp.where(first, solved_b, solved_a)
        tail[rows, :] = dot3(split(solved_a), coupling_a, NN) + dot3(split(solved_b), coupling_b, NN)


def between_chips(value, pairs):
    pairs = [(2 * a + core, 2 * b + core) for a, b in pairs for core in (0, 1)]
    return lax.ppermute(value, "panel", pairs)


def to_other_core(value):
    return lax.ppermute(value, "panel", [(q, q ^ 1) for q in range(lax.axis_size("panel"))])


def gather_rows(value, count):
    shifts = range(1, count)
    return [value] + [lax.ppermute(value, "row", [(j, (j + s) % count) for j in range(count)]) for s in shifts]


def on_device(slab, boundary, diag_inverse, sub_block, tail_coupling, tail_cols):
    panels, count = lax.axis_size("panel"), lax.axis_size("row")
    chips = panels // 2
    chip, core = chip_and_core()
    rows, width = slab.shape
    piece = rows // panels
    held = chips * piece

    def blocks(array, parity):
        array = array.reshape(chips, 2, piece, width)
        return lax.dynamic_index_in_dim(array, parity, 1, keepdims=False).reshape(held, width)

    own = gather_rows(jnp.concatenate([diag_inverse, sub_block]), count)
    keep, got = blocks(slab, core), to_other_core(blocks(slab, 1 - core))
    other = [to_other_core(shard) for shard in own]
    square = (width, width)
    part = (held, width)
    slice_shape = (held // CHUNKS, width)
    own_part, map_a, both, coupling, *carries = call(
        functools.partial(prepare, count, CHUNKS),
        [part, square, square, tail_coupling.shape] + [slice_shape] * CHUNKS,
        [*own, *other, keep, got, blocks(boundary, core), tail_coupling],
        [pltpu.VMEM((2, *square), jnp.float32)] * 2,
        width * width * (3 * width + 4 * held),
    )

    priors, across = None, None
    half = 1
    while True:
        last = 2 * half >= chips
        sources = [s for s in range(half - 1, chips - 1, 2 * half)]
        inner = [s for s in sources if s >= half]
        arrived = []
        for k in range(CHUNKS):
            value = carries[k]
            if priors is not None:
                (value,) = call(inclusive, [slice_shape], [value, priors[k], both], (), width * value.size)
            arrived.append(
                [
                    between_chips(value, [(s, s + 1 + j) for s in sources if s + 1 + j < chips])
                    for j in reversed(range(half))
                ]
            )
        step_map = None
        if not last:
            send = both
            if across is not None:
                (send,) = call(functools.partial(joined, half), [square], [both, across], (), width**3)
            step_map = sum(between_chips(send, [(s, s + 1 + j) for s in inner if s + 1 + j < chips]) for j in range(half))
        if last and priors is not None:
            break
        if priors is None:
            priors = [a[0] for a in arrived]
            across = step_map
        else:
            advanced = functools.partial(advance, half)
            priors = [
                call(advanced, [slice_shape], [priors[k], across, *arrived[k]], (), width * priors[k].size)[0]
                for k in range(CHUNKS)
            ]
            (across,) = call(functools.partial(extend, half), [square], [across, step_map], (), width**3)
        if last:
            arrived = [[] for _ in range(CHUNKS)]
            break
        half *= 2

    own = gather_rows(coupling, count)
    other = [to_other_core(shard) for shard in own]
    arrivals = len(arrived[0])
    stay, leave, tail = call(
        functools.partial(finish, count, CHUNKS, half, arrivals),
        [part] * 3,
        [own_part, map_a, both]
        + ([across] if arrivals else [])
        + [*carries, *priors]
        + [a for chunk in arrived for a in chunk]
        + [*own, *other],
        [pltpu.VMEM((2, *square), jnp.float32), pltpu.VMEM(part, jnp.float32)],
        5 * width * width * held,
    )
    tail = tail.reshape(chips, piece, width)

    def tail_of(index):
        return lax.dynamic_index_in_dim(tail, index, 0, keepdims=False)

    summed = tail_of(chip)
    for shift in reversed(range(1, chips)):
        if chips & (chips - 1) == 0:
            there, pairs = chip ^ shift, [(a, a ^ shift) for a in range(chips)]
        else:
            there, pairs = lax.rem(chip + shift, chips), [(a, (a + shift) % chips) for a in range(chips)]
        summed = summed + between_chips(tail_of(there), pairs)
    came = to_other_core(leave)
    first = core == 0
    parts = [part.reshape(chips, 1, piece, width) for part in (jnp.where(first, stay, came), jnp.where(first, came, stay))]
    factor = jnp.concatenate(parts, axis=1).reshape(rows, width)
    return factor, tail_cols - summed


def solution(mesh):
    placed = (
        P("row", "panel"),
        P("row", None),
        P(("panel", "row"), None),
        P(("panel", "row"), None),
        P(("panel", "row"), None),
        P(("row", "panel"), None),
    )
    return jax.shard_map(
        on_device,
        mesh=mesh,
        in_specs=placed,
        out_specs=(P("row", "panel"), P(("row", "panel"), None)),
        check_vma=False,
    )
```

```python
import functools
import math

import jax
import jax.numpy as jnp
from jax import lax
from jax.experimental import pallas as pl
from jax.experimental.pallas import tpu as pltpu
from jax.sharding import PartitionSpec as P

CHUNKS = 2
NT = (((1,), (1,)), ((), ()))
NN = (((1,), (0,)), ((), ()))
VMEM = pl.BlockSpec(memory_space=pltpu.VMEM)
HBM = pl.BlockSpec(memory_space=pltpu.HBM)
ANY = pl.BlockSpec(memory_space=pl.ANY)


def split(x):
    high = x.astype(jnp.bfloat16)
    return high, (x - high.astype(jnp.float32)).astype(jnp.bfloat16)


def dot3(left, right, dims):
    dot = functools.partial(lax.dot_general, dimension_numbers=dims, preferred_element_type=jnp.float32)
    return dot(left[0], right[0]) + (dot(left[0], right[1]) + dot(left[1], right[0]))


def chip_and_core():
    panel = lax.axis_index("panel")
    return lax.div(panel, 2), lax.rem(panel, 2)


def call(kernel, outs, args, scratch=(), products=0, after=()):
    size = sum(a.size * 4 for a in args) + sum(math.prod(o) * 4 for o in outs)
    inputs = len(args)

    def body(*refs):
        kernel(*refs[:inputs], *refs[inputs + len(after) :])

    return pl.pallas_call(
        body,
        out_shape=[jax.ShapeDtypeStruct(o, jnp.float32) for o in outs],
        in_specs=[VMEM] * inputs + [ANY] * len(after),
        out_specs=[VMEM] * len(outs),
        scratch_shapes=list(scratch),
        compiler_params=pltpu.CompilerParams(vmem_limit_bytes=40 << 20),
        cost_estimate=pl.CostEstimate(flops=6 * products, bytes_accessed=size, transcendentals=0),
    )(*args, *after)


def shard_rows(count, shift, height):
    start = lax.rem(lax.axis_index("row") + count - shift, count) * height
    return pl.ds(pl.multiple_of(start, height), height)


def take(refs, count):
    return [next(refs) for _ in range(count)]


def chunked(ref, chunks, *index):
    height = ref.shape[-2] // chunks
    return [
        ref[(chip, *index, slice(k * height, (k + 1) * height))] for k in range(chunks) for chip in range(ref.shape[0])
    ]


def extract(chunks, slab, bound, kept, entering):
    _, core = chip_and_core()
    kept[...] = jnp.concatenate(chunked(slab, chunks, core))
    entering[...] = jnp.concatenate(chunked(bound, chunks, core))


def prepare(count, chunks, *refs):
    refs = iter(refs)
    own, other = take(refs, count), take(refs, count)
    coupling, given, kept, bound = take(refs, 4)
    map_ref, both_ref, coupling_out = take(refs, 3)
    part_refs, carry_refs = take(refs, chunks), take(refs, chunks)
    inverse, beneath, part = take(refs, 3)
    chip, core = chip_and_core()
    coupling_out[...] = coupling[...]
    height = own[0].shape[0] // 2
    for shift in range(count):
        rows = shard_rows(count, shift, height)
        for slot, shards in ((core, own), (1 - core, other)):
            inverse[slot, rows, :] = shards[shift][:height, :]
            beneath[slot, rows, :] = shards[shift][height:, :]
    inverse_a, inverse_b = split(inverse[0]), split(inverse[1])
    map_a = dot3(inverse_a, split(beneath[0]), NN)
    map_b = dot3(inverse_b, split(beneath[1]), NN)
    parts_a, parts_b = split(map_a), split(map_b)
    map_ref[...] = map_a
    both_ref[...] = dot3(parts_b, parts_a, NN)
    first = core == 0
    got = jnp.concatenate(chunked(given, chunks, core))
    part[...] = dot3(split(jnp.where(first, kept[...], got)), inverse_a, NT)

    @pl.when(chip == 0)
    def _():
        part[...] -= dot3(split(bound[...]), parts_a, NT)

    carry = dot3(split(jnp.where(first, got, kept[...])), inverse_b, NT)
    carry -= dot3(split(part[...]), parts_b, NT)
    height = carry.shape[0] // chunks
    for k in range(chunks):
        rows = slice(k * height, (k + 1) * height)
        part_refs[k][...] = part[rows, :]
        carry_refs[k][...] = carry[rows]


def inclusive(carry, prior, both, out):
    out[...] = carry[...] + dot3(split(prior[...]), split(both[...]), NT)


def absorb(half, prior, across, arrived, put):
    total = arrived[0][...]
    for more in arrived[1:]:
        total = total + more[...]
    chip, _ = chip_and_core()
    inner = lax.rem(chip, half) != 0

    @pl.when(inner)
    def _():
        put(prior[...] + dot3(split(total), split(across[...]), NT))

    @pl.when(jnp.logical_not(inner))
    def _():
        put(prior[...] + total)


def advance(half, prior, across, *refs):
    *arrived, out = refs

    def put(value):
        out[...] = value

    absorb(half, prior, across, arrived, put)


def extend(half, across, arrived, out):
    chip, _ = chip_and_core()
    inner = lax.rem(chip, half) != 0
    upper = lax.rem(chip, 2 * half) >= half
    out[...] = across[...]

    @pl.when(jnp.logical_and(upper, inner))
    def _():
        out[...] = dot3(split(across[...]), split(arrived[...]), NN)

    @pl.when(jnp.logical_and(upper, jnp.logical_not(inner)))
    def _():
        out[...] = arrived[...]


def joined(half, both, across, out):
    chip, _ = chip_and_core()
    out[...] = both[...]

    @pl.when(lax.rem(chip, half) != 0)
    def _():
        out[...] = dot3(split(both[...]), split(across[...]), NN)


def finish(half, arrivals, *refs):
    refs = iter(refs)
    part, carry, prior, map_ref, both = take(refs, 5)
    across = next(refs) if arrivals else None
    arrived = take(refs, arrivals)
    stay, leave, entering = take(refs, 3)
    _, core = chip_and_core()
    first = core == 0

    def put(value):
        entering[...] = value

    if arrivals:
        absorb(half, prior, across, arrived, put)
    else:
        put(prior[...])
    incoming = split(entering[...])
    solved_a = part[...] - dot3(incoming, split(map_ref[...]), NT)
    solved_b = carry[...] + dot3(incoming, split(both[...]), NT)
    stay[...] = jnp.where(first, solved_a, solved_b)
    leave[...] = jnp.where(first, solved_b, solved_a)


def shared(chips, chunks, *refs):
    refs = iter(refs)
    stays, leaves = take(refs, chunks), take(refs, chunks)
    own, other = take(refs, 2)
    outs, tail = take(refs, chips), next(refs)
    chip, _ = chip_and_core()
    own, other = split(own[...]), split(other[...])
    height = stays[0].shape[0] // chips
    for k in range(chunks):
        tail[k] = dot3(split(stays[k][...]), own, NN) + dot3(split(leaves[k][...]), other, NN)
    for shift in range(chips):
        start = pl.multiple_of(destination(chip, shift, chips) * height, height)
        for k in range(chunks):
            outs[shift][k * height : (k + 1) * height, :] = tail[k, pl.ds(start, height), :]


def destination(chip, shift, chips):
    return chip ^ shift if chips & (chips - 1) == 0 else (chip + shift) % chips


def stacked(count, *refs):
    *shards, out = refs
    height = shards[0].shape[0]
    for shift in range(count):
        out[shard_rows(count, shift, height), :] = shards[shift][...]


def interleave(chips, chunks, *refs):
    *sources, out, token, sems = refs
    _, core = chip_and_core()
    height = sources[0].shape[0] // chips
    copies = [
        pltpu.make_async_copy(
            source.at[pl.ds(chip * height, height)],
            out.at[chip, core if at < chunks else 1 - core, pl.ds(at % chunks * height, height)],
            sems.at[at, chip],
        )
        for at, source in enumerate(sources)
        for chip in range(chips)
    ]
    for copy in copies:
        copy.start()
    token[...] = jnp.zeros_like(token)
    for copy in copies:
        copy.wait()


def subtract(cols, *refs):
    *shares, out = refs
    total = shares[0][...]
    for share in shares[1:]:
        total = total + share[...]
    out[...] = cols[...] - total


def between_chips(value, pairs):
    pairs = [(2 * a + core, 2 * b + core) for a, b in pairs for core in (0, 1)]
    return lax.ppermute(value, "panel", pairs)


def to_other_core(value):
    return lax.ppermute(value, "panel", [(q, q ^ 1) for q in range(lax.axis_size("panel"))])


def gather_rows(value, count):
    order = sorted(range(1, count), key=lambda s: min(s, count - s))
    sent = {s: lax.ppermute(value, "row", [(j, (j + s) % count) for j in range(count)]) for s in order}
    return [value] + [sent[s] for s in range(1, count)]


def on_device(slab, boundary, diag_inverse, sub_block, tail_coupling, tail_cols):
    panels, count = lax.axis_size("panel"), lax.axis_size("row")
    chips = panels // 2
    chip, core = chip_and_core()
    rows, width = slab.shape
    piece = rows // panels
    held = chips * piece

    def blocks(array):
        return array.reshape(chips, 2, piece, width)

    own = gather_rows(jnp.concatenate([diag_inverse, sub_block]), count)
    across_slab = to_other_core(slab)
    other = [to_other_core(shard) for shard in own]
    square = (width, width)
    part = (held, width)
    slice_shape = (held // CHUNKS, width)
    kept, bound = call(functools.partial(extract, CHUNKS), [part] * 2, [blocks(slab), blocks(boundary)])
    map_a, both, coupling, *made = call(
        functools.partial(prepare, count, CHUNKS),
        [square, square, tail_coupling.shape] + [slice_shape] * (2 * CHUNKS),
        [*own, *other, tail_coupling, blocks(across_slab), kept, bound],
        [pltpu.VMEM((2, *square), jnp.float32)] * 2 + [pltpu.VMEM(part, jnp.float32)],
        width * width * (3 * width + 4 * held),
    )
    parts, carries = made[:CHUNKS], made[CHUNKS:]

    priors, across = None, None
    half = 1
    while True:
        last = 2 * half >= chips
        sources = [s for s in range(half - 1, chips - 1, 2 * half)]
        inner = [s for s in sources if s >= half]
        arrived = []
        done = []
        for k in range(CHUNKS):
            value = carries[k]
            if priors is not None:
                if k == CHUNKS - 1:
                    done.append(across)
                (value,) = call(inclusive, [slice_shape], [value, priors[k], both], (), width * value.size, after=done)
                done = [value]
            arrived.append(
                [
                    between_chips(value, [(s, s + 1 + j) for s in sources if s + 1 + j < chips])
                    for j in reversed(range(half))
                ]
            )
        step_map = None
        if not last:
            send = both
            if across is not None:
                (send,) = call(functools.partial(joined, half), [square], [both, across], (), width**3)
            step_map = sum(between_chips(send, [(s, s + 1 + j) for s in inner if s + 1 + j < chips]) for j in range(half))
        if last and priors is not None:
            break
        if priors is None:
            priors = [a[0] for a in arrived]
            across = step_map
        else:
            advanced = functools.partial(advance, half)
            priors = [
                call(advanced, [slice_shape], [priors[k], across, *arrived[k]], (), width * priors[k].size)[0]
                for k in range(CHUNKS)
            ]
            (across,) = call(functools.partial(extend, half), [square], [across, step_map], (), width**3)
        if last:
            arrived = [[] for _ in range(CHUNKS)]
            break
        half *= 2

    (own_coupling,) = call(functools.partial(stacked, count), [square], gather_rows(coupling, count), after=[value])
    other_coupling = to_other_core(own_coupling)
    arrivals = len(arrived[0])
    stays, leaves = [], []
    for k in range(CHUNKS):
        stay, leave = call(
            functools.partial(finish, half, arrivals),
            [slice_shape] * 2,
            [parts[k], carries[k], priors[k], map_a, both] + ([across] if arrivals else []) + arrived[k],
            [pltpu.VMEM(slice_shape, jnp.float32)],
            3 * width * width * held // CHUNKS,
            after=stays[-1:],
        )
        stays.append(stay)
        leaves.append(leave)
    shares = call(
        functools.partial(shared, chips, CHUNKS),
        [(piece, width)] * chips,
        [*stays, *leaves, own_coupling, other_coupling],
        [pltpu.VMEM((CHUNKS, *slice_shape), jnp.float32)],
        2 * width * width * held,
    )
    shares = list(shares)
    for k in reversed(range(1, chips)):
        shares[k] = between_chips(shares[k], [(a, destination(a, k, chips)) for a in range(chips)])
    came = [to_other_core(leave) for leave in leaves]
    factor, token = pl.pallas_call(
        functools.partial(interleave, chips, CHUNKS),
        out_shape=[
            jax.ShapeDtypeStruct((chips, 2, piece, width), jnp.float32),
            jax.ShapeDtypeStruct((8, 128), jnp.float32),
        ],
        in_specs=[VMEM] * (2 * CHUNKS),
        out_specs=[HBM, VMEM],
        scratch_shapes=[pltpu.SemaphoreType.DMA((2 * CHUNKS, chips))],
        compiler_params=pltpu.CompilerParams(vmem_limit_bytes=4 << 20),
        cost_estimate=pl.CostEstimate(flops=0, bytes_accessed=16 * held * width, transcendentals=0),
    )(*stays, *came)
    (tail_out,) = call(subtract, [tail_cols.shape], [tail_cols, *shares], after=[token])
    return factor.reshape(rows, width), tail_out


def solution(mesh):
    placed = (
        P("row", "panel"),
        P("row", None),
        P(("panel", "row"), None),
        P(("panel", "row"), None),
        P(("panel", "row"), None),
        P(("row", "panel"), None),
    )
    return jax.shard_map(
        on_device,
        mesh=mesh,
        in_specs=placed,
        out_specs=(P("row", "panel"), P(("row", "panel"), None)),
        check_vma=False,
    )
```

```python
import functools
import math

import jax
import jax.numpy as jnp
from jax import lax
from jax.experimental import pallas as pl
from jax.experimental.pallas import tpu as pltpu
from jax.sharding import PartitionSpec as P

CHUNKS = 2
NT = (((1,), (1,)), ((), ()))
NN = (((1,), (0,)), ((), ()))
VMEM = pl.BlockSpec(memory_space=pltpu.VMEM)
HBM = pl.BlockSpec(memory_space=pltpu.HBM)
ANY = pl.BlockSpec(memory_space=pl.ANY)


def split(x):
    high = x.astype(jnp.bfloat16)
    return high, (x - high.astype(jnp.float32)).astype(jnp.bfloat16)


def dot3(left, right, dims):
    dot = functools.partial(lax.dot_general, dimension_numbers=dims, preferred_element_type=jnp.float32)
    return dot(left[0], right[0]) + (dot(left[0], right[1]) + dot(left[1], right[0]))


def chip_and_core():
    panel = lax.axis_index("panel")
    return lax.div(panel, 2), lax.rem(panel, 2)


def call(kernel, outs, args, scratch=(), products=0, hbm=0, after=()):
    size = sum(a.size * 4 for a in args) + sum(math.prod(o) * 4 for o in outs)
    inputs = len(args)
    args = [*args[: inputs - hbm], *(pltpu.with_memory_space_constraint(a, pltpu.HBM) for a in args[inputs - hbm :])]

    def body(*refs):
        kernel(*refs[:inputs], *refs[inputs + len(after) :])

    return pl.pallas_call(
        body,
        out_shape=[jax.ShapeDtypeStruct(o, jnp.float32) for o in outs],
        in_specs=[VMEM] * (inputs - hbm) + [HBM] * hbm + [ANY] * len(after),
        out_specs=[VMEM] * len(outs),
        scratch_shapes=list(scratch),
        compiler_params=pltpu.CompilerParams(vmem_limit_bytes=40 << 20),
        cost_estimate=pl.CostEstimate(flops=6 * products, bytes_accessed=size, transcendentals=0),
    )(*args, *after)


def shifts(count):
    return [0] + sorted(range(1, count), key=lambda s: (min(s, count - s), s))


def shard_rows(count, shift, height):
    start = lax.rem(lax.axis_index("row") + count - shift, count) * height
    return pl.ds(pl.multiple_of(start, height), height)


def take(refs, count):
    return [next(refs) for _ in range(count)]


def chunked(ref, chunks, *index):
    height = ref.shape[-2] // chunks
    return jnp.concatenate(
        [ref[(chip, *index, slice(k * height, (k + 1) * height))] for k in range(chunks) for chip in range(ref.shape[0])]
    )


def prepare(count, chunks, *refs):
    refs = iter(refs)
    own, other = take(refs, count), take(refs, count)
    given, coupling, slab, bound = take(refs, 4)
    map_ref, both_ref, coupling_out = take(refs, 3)
    part_refs, carry_refs = take(refs, chunks), take(refs, chunks)
    inverse, beneath, part, kept, entering, sems = take(refs, 6)
    chip, core = chip_and_core()
    slab_copy = pltpu.make_async_copy(slab.at[:, core], kept, sems.at[0])
    bound_copy = pltpu.make_async_copy(bound.at[:, core], entering, sems.at[1])
    coupling_copy = pltpu.make_async_copy(coupling, coupling_out, sems.at[2])
    slab_copy.start()

    @pl.when(chip == 0)
    def _():
        bound_copy.start()

    coupling_copy.start()
    height = own[0].shape[0] // 2
    for at, shift in enumerate(shifts(count)):
        rows = shard_rows(count, shift, height)
        for slot, shards in ((core, own), (1 - core, other)):
            inverse[slot, rows, :] = shards[at][:height, :]
            beneath[slot, rows, :] = shards[at][height:, :]
    inverse_a, inverse_b = split(inverse[0]), split(inverse[1])
    map_a = dot3(inverse_a, split(beneath[0]), NN)
    map_b = dot3(inverse_b, split(beneath[1]), NN)
    parts_a, parts_b = split(map_a), split(map_b)
    map_ref[...] = map_a
    both_ref[...] = dot3(parts_b, parts_a, NN)
    first = core == 0
    got = chunked(given, chunks, core)
    slab_copy.wait()
    keep = chunked(kept, chunks)
    part[...] = dot3(split(jnp.where(first, keep, got)), inverse_a, NT)

    @pl.when(chip == 0)
    def _():
        bound_copy.wait()
        part[...] -= dot3(split(chunked(entering, chunks)), parts_a, NT)

    carry = dot3(split(jnp.where(first, got, keep)), inverse_b, NT)
    carry -= dot3(split(part[...]), parts_b, NT)
    height = carry.shape[0] // chunks
    for k in range(chunks):
        rows = slice(k * height, (k + 1) * height)
        part_refs[k][...] = part[rows, :]
        carry_refs[k][...] = carry[rows]
    coupling_copy.wait()


def inclusive(carry, prior, both, out):
    out[...] = carry[...] + dot3(split(prior[...]), split(both[...]), NT)


def absorb(half, prior, across, arrived, put):
    total = arrived[0][...]
    for more in arrived[1:]:
        total = total + more[...]
    chip, _ = chip_and_core()
    inner = lax.rem(chip, half) != 0

    @pl.when(inner)
    def _():
        put(prior[...] + dot3(split(total), split(across[...]), NT))

    @pl.when(jnp.logical_not(inner))
    def _():
        put(prior[...] + total)


def advance(half, prior, across, *refs):
    *arrived, out = refs

    def put(value):
        out[...] = value

    absorb(half, prior, across, arrived, put)


def extend(half, across, arrived, out):
    chip, _ = chip_and_core()
    inner = lax.rem(chip, half) != 0
    upper = lax.rem(chip, 2 * half) >= half
    out[...] = across[...]

    @pl.when(jnp.logical_and(upper, inner))
    def _():
        out[...] = dot3(split(across[...]), split(arrived[...]), NN)

    @pl.when(jnp.logical_and(upper, jnp.logical_not(inner)))
    def _():
        out[...] = arrived[...]


def joined(half, both, across, out):
    chip, _ = chip_and_core()
    out[...] = both[...]

    @pl.when(lax.rem(chip, half) != 0)
    def _():
        out[...] = dot3(split(both[...]), split(across[...]), NN)


def finish(half, arrivals, *refs):
    refs = iter(refs)
    part, carry, prior, map_ref, both = take(refs, 5)
    across = next(refs) if arrivals else None
    arrived = take(refs, arrivals)
    stay, leave, entering = take(refs, 3)
    _, core = chip_and_core()
    first = core == 0

    def put(value):
        entering[...] = value

    if arrivals:
        absorb(half, prior, across, arrived, put)
    else:
        put(prior[...])
    incoming = split(entering[...])
    solved_a = part[...] - dot3(incoming, split(map_ref[...]), NT)
    solved_b = carry[...] + dot3(incoming, split(both[...]), NT)
    stay[...] = jnp.where(first, solved_a, solved_b)
    leave[...] = jnp.where(first, solved_b, solved_a)


def shared(chips, chunks, *refs):
    refs = iter(refs)
    stays, leaves = take(refs, chunks), take(refs, chunks)
    own, other = take(refs, 2)
    outs, tail = take(refs, chips), next(refs)
    chip, _ = chip_and_core()
    own, other = split(own[...]), split(other[...])
    height = stays[0].shape[0] // chips
    for k in range(chunks):
        tail[k] = dot3(split(stays[k][...]), own, NN) + dot3(split(leaves[k][...]), other, NN)
    for shift in range(chips):
        start = pl.multiple_of(destination(chip, shift, chips) * height, height)
        for k in range(chunks):
            outs[shift][k * height : (k + 1) * height, :] = tail[k, pl.ds(start, height), :]


def destination(chip, shift, chips):
    return chip ^ shift if chips & (chips - 1) == 0 else (chip + shift) % chips


def stacked(count, *refs):
    *shards, out = refs
    height = shards[0].shape[0]
    for at, shift in enumerate(shifts(count)):
        out[shard_rows(count, shift, height), :] = shards[at][...]


def interleave(chips, chunks, *refs):
    *sources, out, token, sems = refs
    _, core = chip_and_core()
    height = sources[0].shape[0] // chips
    copies = [
        pltpu.make_async_copy(
            source.at[pl.ds(chip * height, height)],
            out.at[chip, core if at < chunks else 1 - core, pl.ds(at % chunks * height, height)],
            sems.at[at, chip],
        )
        for at, source in enumerate(sources)
        for chip in range(chips)
    ]
    for copy in copies:
        copy.start()
    token[...] = jnp.zeros_like(token)
    for copy in copies:
        copy.wait()


def subtract(cols, *refs):
    *shares, out = refs
    total = shares[0][...]
    for share in shares[1:]:
        total = total + share[...]
    out[...] = cols[...] - total


def between_chips(value, pairs):
    pairs = [(2 * a + core, 2 * b + core) for a, b in pairs for core in (0, 1)]
    return lax.ppermute(value, "panel", pairs)


def to_other_core(value):
    return lax.ppermute(value, "panel", [(q, q ^ 1) for q in range(lax.axis_size("panel"))])


def gather_rows(value, count):
    moved = [lax.ppermute(value, "row", [(j, (j + s) % count) for j in range(count)]) for s in shifts(count)[1:]]
    return [value, *moved]


def on_device(slab, boundary, diag_inverse, sub_block, tail_coupling, tail_cols):
    panels, count = lax.axis_size("panel"), lax.axis_size("row")
    chips = panels // 2
    chip, core = chip_and_core()
    rows, width = slab.shape
    piece = rows // panels
    held = chips * piece

    def blocks(array):
        return array.reshape(chips, 2, piece, width)

    own = gather_rows(jnp.concatenate([diag_inverse, sub_block]), count)
    across_slab = to_other_core(slab)
    other = [to_other_core(shard) for shard in own]
    square = (width, width)
    part = (held, width)
    slice_shape = (held // CHUNKS, width)
    map_a, both, coupling, *made = call(
        functools.partial(prepare, count, CHUNKS),
        [square, square, tail_coupling.shape] + [slice_shape] * (2 * CHUNKS),
        [*own, *other, blocks(across_slab), tail_coupling, blocks(slab), blocks(boundary)],
        [pltpu.VMEM((2, *square), jnp.float32)] * 2
        + [pltpu.VMEM(part, jnp.float32)]
        + [pltpu.VMEM((chips, piece, width), jnp.float32)] * 2
        + [pltpu.SemaphoreType.DMA((3,))],
        width * width * (3 * width + 4 * held),
        hbm=3,
    )
    parts, carries = made[:CHUNKS], made[CHUNKS:]

    def spread(after):
        return call(functools.partial(stacked, count), [square], gather_rows(coupling, count), after=after)[0]

    own_coupling = None
    priors, across = None, None
    half = 1
    while True:
        last = 2 * half >= chips
        sources = [s for s in range(half - 1, chips - 1, 2 * half)]
        inner = [s for s in sources if s >= half]
        arrived = []
        done = []
        for k in range(CHUNKS):
            value = carries[k]
            if priors is not None:
                if k == CHUNKS - 1 and last:
                    own_coupling = spread(done)
                    done.append(own_coupling)
                (value,) = call(inclusive, [slice_shape], [value, priors[k], both], (), width * value.size, after=done)
                done = [value]
            arrived.append(
                [
                    between_chips(value, [(s, s + 1 + j) for s in sources if s + 1 + j < chips])
                    for j in reversed(range(half))
                ]
            )
        step_map = None
        if not last:
            send = both
            if across is not None:
                (send,) = call(functools.partial(joined, half), [square], [both, across], (), width**3)
            step_map = sum(between_chips(send, [(s, s + 1 + j) for s in inner if s + 1 + j < chips]) for j in range(half))
        if last and priors is not None:
            break
        if priors is None:
            priors = [a[0] for a in arrived]
            across = step_map
        else:
            advanced = functools.partial(advance, half)
            priors = [
                call(advanced, [slice_shape], [priors[k], across, *arrived[k]], (), width * priors[k].size)[0]
                for k in range(CHUNKS)
            ]
            (across,) = call(functools.partial(extend, half), [square], [across, step_map], (), width**3)
        if last:
            arrived = [[] for _ in range(CHUNKS)]
            break
        half *= 2

    if own_coupling is None:
        own_coupling = spread([])
    other_coupling = to_other_core(own_coupling)
    arrivals = len(arrived[0])
    stays, leaves = [], []
    for k in range(CHUNKS):
        stay, leave = call(
            functools.partial(finish, half, arrivals),
            [slice_shape] * 2,
            [parts[k], carries[k], priors[k], map_a, both] + ([across] if arrivals else []) + arrived[k],
            [pltpu.VMEM(slice_shape, jnp.float32)],
            3 * width * width * held // CHUNKS,
            after=stays[-1:],
        )
        stays.append(stay)
        leaves.append(leave)
    shares = call(
        functools.partial(shared, chips, CHUNKS),
        [(piece, width)] * chips,
        [*stays, *leaves, own_coupling, other_coupling],
        [pltpu.VMEM((CHUNKS, *slice_shape), jnp.float32)],
        2 * width * width * held,
    )
    shares = list(shares)
    for k in reversed(range(1, chips)):
        shares[k] = between_chips(shares[k], [(a, destination(a, k, chips)) for a in range(chips)])
    came = [to_other_core(leave) for leave in leaves]
    factor, token = pl.pallas_call(
        functools.partial(interleave, chips, CHUNKS),
        out_shape=[
            jax.ShapeDtypeStruct((chips, 2, piece, width), jnp.float32),
            jax.ShapeDtypeStruct((8, 128), jnp.float32),
        ],
        in_specs=[VMEM] * (2 * CHUNKS),
        out_specs=[HBM, VMEM],
        scratch_shapes=[pltpu.SemaphoreType.DMA((2 * CHUNKS, chips))],
        compiler_params=pltpu.CompilerParams(vmem_limit_bytes=4 << 20),
        cost_estimate=pl.CostEstimate(flops=0, bytes_accessed=16 * held * width, transcendentals=0),
    )(*stays, *came)
    (tail_out,) = call(subtract, [tail_cols.shape], [tail_cols, *shares], after=[token])
    return factor.reshape(rows, width), tail_out


def solution(mesh):
    placed = (
        P("row", "panel"),
        P("row", None),
        P(("panel", "row"), None),
        P(("panel", "row"), None),
        P(("panel", "row"), None),
        P(("row", "panel"), None),
    )
    return jax.shard_map(
        on_device,
        mesh=mesh,
        in_specs=placed,
        out_specs=(P("row", "panel"), P(("row", "panel"), None)),
        check_vma=False,
    )
```

```python
import functools
import math

import jax
import jax.numpy as jnp
from jax import lax
from jax.experimental import pallas as pl
from jax.experimental.pallas import tpu as pltpu
from jax.sharding import PartitionSpec as P

CHUNKS = 2
FIRST = 1 / 2
NT = (((1,), (1,)), ((), ()))
NN = (((1,), (0,)), ((), ()))
VMEM = pl.BlockSpec(memory_space=pltpu.VMEM)
HBM = pl.BlockSpec(memory_space=pltpu.HBM)
ANY = pl.BlockSpec(memory_space=pl.ANY)


def split(x):
    high = x.astype(jnp.bfloat16)
    return high, (x - high.astype(jnp.float32)).astype(jnp.bfloat16)


def dot3(left, right, dims):
    dot = functools.partial(lax.dot_general, dimension_numbers=dims, preferred_element_type=jnp.float32)
    return dot(left[0], right[0]) + (dot(left[0], right[1]) + dot(left[1], right[0]))


def chip_and_core():
    panel = lax.axis_index("panel")
    return lax.div(panel, 2), lax.rem(panel, 2)


def call(kernel, outs, args, scratch=(), products=0, hbm=0, after=()):
    size = sum(a.size * 4 for a in args) + sum(math.prod(o) * 4 for o in outs)
    inputs = len(args)
    args = [*args[: inputs - hbm], *(pltpu.with_memory_space_constraint(a, pltpu.HBM) for a in args[inputs - hbm :])]

    def body(*refs):
        kernel(*refs[:inputs], *refs[inputs + len(after) :])

    return pl.pallas_call(
        body,
        out_shape=[jax.ShapeDtypeStruct(o, jnp.float32) for o in outs],
        in_specs=[VMEM] * (inputs - hbm) + [HBM] * hbm + [ANY] * len(after),
        out_specs=[VMEM] * len(outs),
        scratch_shapes=list(scratch),
        compiler_params=pltpu.CompilerParams(vmem_limit_bytes=40 << 20),
        cost_estimate=pl.CostEstimate(flops=6 * products, bytes_accessed=size, transcendentals=0),
    )(*args, *after)


def weight_shifts(count):
    return sorted(range(count), key=lambda s: (min(s, count - s), s))


def shard_rows(count, shift, height):
    start = lax.rem(lax.axis_index("row") + count - shift, count) * height
    return pl.ds(pl.multiple_of(start, height), height)


def take(refs, count):
    return [next(refs) for _ in range(count)]


def cuts(piece):
    unit = 16 if piece % 16 == 0 and piece > 16 else 8
    first = max(unit, int(piece * FIRST) // unit * unit)
    if piece % unit or first >= piece:
        first = piece // 2
    return [(0, first), (first, piece)]


def chunked(ref, *index):
    return jnp.concatenate(
        [ref[(chip, *index, slice(*cut))] for cut in cuts(ref.shape[-2]) for chip in range(ref.shape[0])]
    )


def fetch(slab, bound, coupling, kept, entering, coupling_out, sems):
    _, core = chip_and_core()
    copies = [
        pltpu.make_async_copy(source, target, sems.at[k])
        for k, (source, target) in enumerate(
            ((slab.at[:, core], kept), (bound.at[:, core], entering), (coupling, coupling_out))
        )
    ]
    for copy in copies:
        copy.start()
    for copy in copies:
        copy.wait()


def prepare(count, *refs):
    refs = iter(refs)
    own, other = take(refs, count), take(refs, count)
    given, kept, entering, coupling = take(refs, 4)
    map_ref, both_ref, coupling_out = take(refs, 3)
    part_refs, carry_refs = take(refs, CHUNKS), take(refs, CHUNKS)
    inverse, beneath, part = take(refs, 3)
    chip, core = chip_and_core()
    coupling_out[...] = coupling[...]
    height = own[0].shape[0] // 2
    for at, shift in enumerate(weight_shifts(count)):
        rows = shard_rows(count, shift, height)
        for slot, shards in ((core, own), (1 - core, other)):
            inverse[slot, rows, :] = shards[at][:height, :]
            beneath[slot, rows, :] = shards[at][height:, :]
    inverse_a, inverse_b = split(inverse[0]), split(inverse[1])
    map_ref[...] = dot3(inverse_a, split(beneath[0]), NN)
    map_a = split(map_ref[...])
    map_b = split(dot3(inverse_b, split(beneath[1]), NN))
    both_ref[...] = dot3(map_b, map_a, NN)
    first = core == 0
    got, keep = chunked(given, core), chunked(kept)
    part[...] = dot3(split(jnp.where(first, keep, got)), inverse_a, NT)

    @pl.when(chip == 0)
    def _():
        part[...] -= dot3(split(chunked(entering)), map_a, NT)

    carry = dot3(split(jnp.where(first, got, keep)), inverse_b, NT)
    carry -= dot3(split(part[...]), map_b, NT)
    start = 0
    for k in range(CHUNKS):
        end = start + part_refs[k].shape[0]
        part_refs[k][...] = part[start:end, :]
        carry_refs[k][...] = carry[start:end]
        start = end


def inclusive(carry, prior, both, out):
    out[...] = carry[...] + dot3(split(prior[...]), split(both[...]), NT)


def total(refs):
    value = refs[0][...]
    for more in refs[1:]:
        value = value + more[...]
    return value


def absorb(half, prior, across, arrived, put):
    chip, _ = chip_and_core()
    inner = lax.rem(chip, half) != 0

    @pl.when(inner)
    def _():
        put(prior[...] + dot3(split(total(arrived)), split(across[...]), NT))

    @pl.when(jnp.logical_not(inner))
    def _():
        put(prior[...] + total(arrived))


def advance(half, prior, across, *refs):
    *arrived, out = refs

    def put(value):
        out[...] = value

    absorb(half, prior, across, arrived, put)


def extend(half, across, arrived, out):
    chip, _ = chip_and_core()
    inner = lax.rem(chip, half) != 0
    upper = lax.rem(chip, 2 * half) >= half
    out[...] = across[...]

    @pl.when(jnp.logical_and(upper, inner))
    def _():
        out[...] = dot3(split(across[...]), split(arrived[...]), NN)

    @pl.when(jnp.logical_and(upper, jnp.logical_not(inner)))
    def _():
        out[...] = arrived[...]


def joined(half, both, across, out):
    chip, _ = chip_and_core()
    out[...] = both[...]

    @pl.when(lax.rem(chip, half) != 0)
    def _():
        out[...] = dot3(split(both[...]), split(across[...]), NN)


def finish(half, arrivals, *refs):
    refs = iter(refs)
    part, carry, map_ref, both = take(refs, 4)
    across = next(refs) if arrivals else None
    prior = next(refs)
    arrived = take(refs, arrivals)
    stay, leave, entering = take(refs, 3)
    _, core = chip_and_core()
    first = core == 0

    def put(value):
        entering[...] = value

    if arrivals:
        absorb(half, prior, across, arrived, put)
    else:
        put(prior[...])
    incoming = split(entering[...])
    solved_a = part[...] - dot3(incoming, split(map_ref[...]), NT)
    solved_b = carry[...] + dot3(incoming, split(both[...]), NT)
    stay[...] = jnp.where(first, solved_a, solved_b)
    leave[...] = jnp.where(first, solved_b, solved_a)


def shared(chips, *refs):
    refs = iter(refs)
    stays, leaves = take(refs, CHUNKS), take(refs, CHUNKS)
    own, other = take(refs, 2)
    outs, tails = take(refs, chips), take(refs, CHUNKS)
    chip, _ = chip_and_core()
    own, other = split(own[...]), split(other[...])
    for k in range(CHUNKS):
        tails[k][...] = dot3(split(stays[k][...]), own, NN) + dot3(split(leaves[k][...]), other, NN)
    for shift in range(chips):
        for k, (begin, end) in enumerate(cuts(outs[0].shape[0])):
            height = end - begin
            start = pl.multiple_of(destination(chip, shift, chips) * height, height)
            outs[shift][begin:end, :] = tails[k][pl.ds(start, height), :]


def destination(chip, shift, chips):
    return chip ^ shift if chips & (chips - 1) == 0 else (chip + shift) % chips


def stacked(count, *refs):
    *shards, out = refs
    height = shards[0].shape[0]
    for shift in range(count):
        out[shard_rows(count, shift, height), :] = shards[shift][...]


def interleave(*refs):
    *sources, out, token, sems = refs
    _, core = chip_and_core()
    copies = []
    for at, source in enumerate(sources):
        begin, end = cuts(out.shape[2])[at % CHUNKS]
        height = end - begin
        for chip in range(out.shape[0]):
            target = out.at[chip, core if at < CHUNKS else 1 - core, pl.ds(begin, height)]
            copies.append(pltpu.make_async_copy(source.at[pl.ds(chip * height, height)], target, sems.at[at, chip]))
    for copy in copies:
        copy.start()
    token[...] = jnp.zeros_like(token)
    for copy in copies:
        copy.wait()


def subtract(cols, *refs):
    *shares, out = refs
    total = shares[0][...]
    for share in shares[1:]:
        total = total + share[...]
    out[...] = cols[...] - total


def between_chips(value, pairs):
    pairs = [(2 * a + core, 2 * b + core) for a, b in pairs for core in (0, 1)]
    return lax.ppermute(value, "panel", pairs)


def to_other_core(value):
    return lax.ppermute(value, "panel", [(q, q ^ 1) for q in range(lax.axis_size("panel"))])


def gather_rows(value, order):
    count = lax.axis_size("row")
    moved = [lax.ppermute(value, "row", [(j, (j + s) % count) for j in range(count)]) for s in order if s]
    return [value, *moved]


def on_device(slab, boundary, diag_inverse, sub_block, tail_coupling, tail_cols):
    panels, count = lax.axis_size("panel"), lax.axis_size("row")
    chips = panels // 2
    chip, core = chip_and_core()
    rows, width = slab.shape
    piece = rows // panels
    held = chips * piece

    def blocks(array):
        return array.reshape(chips, 2, piece, width)

    own = gather_rows(jnp.concatenate([diag_inverse, sub_block]), weight_shifts(count))
    across_slab = to_other_core(slab)
    other = [to_other_core(shard) for shard in own]
    square = (width, width)
    part = (held, width)
    slices = [(chips * (end - begin), width) for begin, end in cuts(piece)]
    three = (chips, piece, width)
    kept, entering, coupling = call(
        fetch,
        [three, three, tail_coupling.shape],
        [blocks(slab), blocks(boundary), tail_coupling],
        [pltpu.SemaphoreType.DMA((3,))],
        hbm=3,
    )
    map_a, both, coupling, *made = call(
        functools.partial(prepare, count),
        [square, square, tail_coupling.shape] + slices * 2,
        [*own, *other, blocks(across_slab), kept, entering, coupling],
        [pltpu.VMEM((2, *square), jnp.float32)] * 2 + [pltpu.VMEM(part, jnp.float32)],
        width * width * (3 * width + 4 * held),
    )
    parts, carries = made[:CHUNKS], made[CHUNKS:]

    def spread(after):
        shards = gather_rows(coupling, range(count))
        return call(functools.partial(stacked, count), [square], shards, after=after)[0]

    def send_map(value, groups):
        return sum(between_chips(value, group) for group in groups if group)

    own_coupling = None
    priors, across = None, None
    half = 1
    while True:
        last = 2 * half >= chips
        sources = [s for s in range(half - 1, chips - 1, 2 * half)]
        pairs = [[(s, s + 1 + j) for s in sources if s + 1 + j < chips] for j in range(half)]
        maps = [[(s, t) for s, t in group if s >= half] for group in pairs]
        arrived, done = [], []
        for k in range(CHUNKS):
            value = carries[k]
            if priors is not None:
                if k == CHUNKS - 1 and half == 2:
                    own_coupling = spread(done)
                    done = [*done, own_coupling]
                (value,) = call(inclusive, [slices[k]], [value, priors[k], both], (), width * value.size, after=done)
                done = [value]
            arrived.append([between_chips(value, group) for group in reversed(pairs)])
        if last and priors is not None:
            break
        if priors is None:
            priors = [a[0] for a in arrived]
            if any(maps):
                across = send_map(both, maps)
        else:
            (send,) = call(functools.partial(joined, half), [square], [both, across], (), width**3)
            step_map = send_map(send, maps)
            priors = [
                call(
                    functools.partial(advance, half),
                    [slices[k]],
                    [priors[k], across, *arrived[k]],
                    (),
                    width * priors[k].size,
                )[0]
                for k in range(CHUNKS)
            ]
            (across,) = call(functools.partial(extend, half), [square], [across, step_map], (), width**3)
        if last:
            arrived = [[] for _ in range(CHUNKS)]
            break
        half *= 2

    if own_coupling is None:
        own_coupling = spread([])
    other_coupling = to_other_core(own_coupling)
    arrivals = len(arrived[0])
    stays, leaves = [], []
    for k in range(CHUNKS):
        stay, leave = call(
            functools.partial(finish, half, arrivals),
            [slices[k]] * 2,
            [parts[k], carries[k], map_a, both] + ([across] if arrivals else []) + [priors[k], *arrived[k]],
            [pltpu.VMEM(slices[k], jnp.float32)],
            3 * width * parts[k].size,
            after=stays[-1:],
        )
        stays.append(stay)
        leaves.append(leave)
    shares = call(
        functools.partial(shared, chips),
        [(piece, width)] * chips,
        [*stays, *leaves, own_coupling, other_coupling],
        [pltpu.VMEM(shape, jnp.float32) for shape in slices],
        2 * width * width * held,
    )
    shares = list(shares)
    for k in reversed(range(1, chips)):
        shares[k] = between_chips(shares[k], [(a, destination(a, k, chips)) for a in range(chips)])
    came = [to_other_core(leave) for leave in leaves]
    factor, token = pl.pallas_call(
        interleave,
        out_shape=[
            jax.ShapeDtypeStruct((chips, 2, piece, width), jnp.float32),
            jax.ShapeDtypeStruct((8, 128), jnp.float32),
        ],
        in_specs=[VMEM] * (2 * CHUNKS),
        out_specs=[HBM, VMEM],
        scratch_shapes=[pltpu.SemaphoreType.DMA((2 * CHUNKS, chips))],
        compiler_params=pltpu.CompilerParams(vmem_limit_bytes=4 << 20),
        cost_estimate=pl.CostEstimate(flops=0, bytes_accessed=16 * held * width, transcendentals=0),
    )(*stays, *came)
    (tail_out,) = call(subtract, [tail_cols.shape], [tail_cols, *shares], after=[token])
    return factor.reshape(rows, width), tail_out


def solution(mesh):
    placed = (
        P("row", "panel"),
        P("row", None),
        P(("panel", "row"), None),
        P(("panel", "row"), None),
        P(("panel", "row"), None),
        P(("row", "panel"), None),
    )
    return jax.shard_map(
        on_device,
        mesh=mesh,
        in_specs=placed,
        out_specs=(P("row", "panel"), P(("row", "panel"), None)),
        check_vma=False,
    )
```

```python
import functools
import math

import jax
import jax.numpy as jnp
from jax import lax
from jax.experimental import pallas as pl
from jax.experimental.pallas import tpu as pltpu
from jax.sharding import PartitionSpec as P

CHUNKS = 2
FIRST = 1 / 2
SCAN_SPAN = 2_000_000_000
FINISH_SPAN = 4_000_000_000
NT = (((1,), (1,)), ((), ()))
NN = (((1,), (0,)), ((), ()))
VMEM = pl.BlockSpec(memory_space=pltpu.VMEM)
HBM = pl.BlockSpec(memory_space=pltpu.HBM)
ANY = pl.BlockSpec(memory_space=pl.ANY)


def split(x):
    high = x.astype(jnp.bfloat16)
    return high, (x - high.astype(jnp.float32)).astype(jnp.bfloat16)


def dot3(left, right, dims):
    dot = functools.partial(lax.dot_general, dimension_numbers=dims, preferred_element_type=jnp.float32)
    return dot(left[0], right[0]) + (dot(left[0], right[1]) + dot(left[1], right[0]))


def chip_and_core():
    panel = lax.axis_index("panel")
    return lax.div(panel, 2), lax.rem(panel, 2)


def call(kernel, outs, args, scratch=(), span=0, hbm=0, after=()):
    size = sum(a.size * 4 for a in args) + sum(math.prod(o) * 4 for o in outs)
    inputs = len(args)
    args = [*args[: inputs - hbm], *(pltpu.with_memory_space_constraint(a, pltpu.HBM) for a in args[inputs - hbm :])]

    def body(*refs):
        kernel(*refs[:inputs], *refs[inputs + len(after) :])

    return pl.pallas_call(
        body,
        out_shape=[jax.ShapeDtypeStruct(o, jnp.float32) for o in outs],
        in_specs=[VMEM] * (inputs - hbm) + [HBM] * hbm + [ANY] * len(after),
        out_specs=[VMEM] * len(outs),
        scratch_shapes=list(scratch),
        compiler_params=pltpu.CompilerParams(vmem_limit_bytes=40 << 20),
        cost_estimate=pl.CostEstimate(flops=2 * span, bytes_accessed=size, transcendentals=0),
    )(*args, *after)


def weight_shifts(count):
    return [0, *reversed(range(1, count))]


def shard_rows(count, shift, height):
    start = lax.rem(lax.axis_index("row") + count - shift, count) * height
    return pl.ds(pl.multiple_of(start, height), height)


def take(refs, count):
    return [next(refs) for _ in range(count)]


def cuts(piece):
    unit = 16 if piece % 16 == 0 and piece > 16 else 8
    first = max(unit, int(piece * FIRST) // unit * unit)
    if piece % unit or first >= piece:
        first = piece // 2
    return [(0, first), (first, piece)]


def chunked(ref, *index):
    return jnp.concatenate(
        [ref[(chip, *index, slice(*cut))] for cut in cuts(ref.shape[-2]) for chip in range(ref.shape[0])]
    )


def fetch(slab, bound, coupling, kept, entering, coupling_out, sems):
    _, core = chip_and_core()
    copies = [
        pltpu.make_async_copy(source, target, sems.at[k])
        for k, (source, target) in enumerate(
            ((slab.at[:, core], kept), (bound.at[:, core], entering), (coupling, coupling_out))
        )
    ]
    for copy in copies:
        copy.start()
    for copy in copies:
        copy.wait()


def prepare(count, *refs):
    refs = iter(refs)
    own, other = take(refs, count), take(refs, count)
    given, kept, entering, coupling = take(refs, 4)
    map_ref, both_ref, coupling_out = take(refs, 3)
    part_refs, carry_refs = take(refs, CHUNKS), take(refs, CHUNKS)
    inverse, beneath, part = take(refs, 3)
    chip, core = chip_and_core()
    coupling_out[...] = coupling[...]
    height = own[0].shape[0] // 2
    for at, shift in enumerate(weight_shifts(count)):
        rows = shard_rows(count, shift, height)
        for slot, shards in ((core, own), (1 - core, other)):
            inverse[slot, rows, :] = shards[at][:height, :]
            beneath[slot, rows, :] = shards[at][height:, :]
    inverse_a, inverse_b = split(inverse[0]), split(inverse[1])
    map_ref[...] = dot3(inverse_a, split(beneath[0]), NN)
    map_a = split(map_ref[...])
    map_b = split(dot3(inverse_b, split(beneath[1]), NN))
    both_ref[...] = dot3(map_b, map_a, NN)
    first = core == 0
    got, keep = chunked(given, core), chunked(kept)
    part[...] = dot3(split(jnp.where(first, keep, got)), inverse_a, NT)

    @pl.when(chip == 0)
    def _():
        part[...] -= dot3(split(chunked(entering)), map_a, NT)

    carry = dot3(split(jnp.where(first, got, keep)), inverse_b, NT)
    carry -= dot3(split(part[...]), map_b, NT)
    start = 0
    for k in range(CHUNKS):
        end = start + part_refs[k].shape[0]
        part_refs[k][...] = part[start:end, :]
        carry_refs[k][...] = carry[start:end]
        start = end


def inclusive(carry, prior, both, out):
    out[...] = carry[...] + dot3(split(prior[...]), split(both[...]), NT)


def total(refs):
    value = refs[0][...]
    for more in refs[1:]:
        value = value + more[...]
    return value


def absorb(half, prior, across, arrived, put):
    chip, _ = chip_and_core()
    inner = lax.rem(chip, half) != 0

    @pl.when(inner)
    def _():
        put(prior[...] + dot3(split(total(arrived)), split(across[...]), NT))

    @pl.when(jnp.logical_not(inner))
    def _():
        put(prior[...] + total(arrived))


def advance(half, prior, across, *refs):
    *arrived, out = refs

    def put(value):
        out[...] = value

    absorb(half, prior, across, arrived, put)


def extend(half, across, arrived, out):
    chip, _ = chip_and_core()
    inner = lax.rem(chip, half) != 0
    upper = lax.rem(chip, 2 * half) >= half
    out[...] = across[...]

    @pl.when(jnp.logical_and(upper, inner))
    def _():
        out[...] = dot3(split(across[...]), split(arrived[...]), NN)

    @pl.when(jnp.logical_and(upper, jnp.logical_not(inner)))
    def _():
        out[...] = arrived[...]


def joined(half, both, across, out):
    chip, _ = chip_and_core()
    out[...] = both[...]

    @pl.when(lax.rem(chip, half) != 0)
    def _():
        out[...] = dot3(split(both[...]), split(across[...]), NN)


def finish(half, arrivals, *refs):
    refs = iter(refs)
    part, carry, map_ref, both = take(refs, 4)
    across = next(refs) if arrivals else None
    prior = next(refs)
    arrived = take(refs, arrivals)
    stay, leave, entering = take(refs, 3)
    _, core = chip_and_core()
    first = core == 0

    def put(value):
        entering[...] = value

    if arrivals:
        absorb(half, prior, across, arrived, put)
    else:
        put(prior[...])
    incoming = split(entering[...])
    solved_a = part[...] - dot3(incoming, split(map_ref[...]), NT)
    solved_b = carry[...] + dot3(incoming, split(both[...]), NT)
    stay[...] = jnp.where(first, solved_a, solved_b)
    leave[...] = jnp.where(first, solved_b, solved_a)


def shared(chips, *refs):
    refs = iter(refs)
    stays, leaves = take(refs, CHUNKS), take(refs, CHUNKS)
    own, other = take(refs, 2)
    outs, tails = take(refs, chips), take(refs, CHUNKS)
    chip, _ = chip_and_core()
    own, other = split(own[...]), split(other[...])
    for k in range(CHUNKS):
        tails[k][...] = dot3(split(stays[k][...]), own, NN) + dot3(split(leaves[k][...]), other, NN)
    for shift in range(chips):
        for k, (begin, end) in enumerate(cuts(outs[0].shape[0])):
            height = end - begin
            start = pl.multiple_of(destination(chip, shift, chips) * height, height)
            outs[shift][begin:end, :] = tails[k][pl.ds(start, height), :]


def destination(chip, shift, chips):
    return chip ^ shift if chips & (chips - 1) == 0 else (chip + shift) % chips


def packed(*refs):
    *sources, out = refs
    at = 0
    for source in sources:
        out[at : at + source.shape[0], :] = source[...]
        at += source.shape[0]


def stacked(count, *refs):
    *sources, out = refs
    row = lax.axis_index("row")
    height = out.shape[0] // count
    at = 0
    for source in sources:
        for k in range(source.shape[0] // height):
            start = pl.multiple_of((row ^ at) * height, height)
            out[pl.ds(start, height), :] = source[k * height : (k + 1) * height, :]
            at += 1


def interleave(*refs):
    *sources, out, token, sems = refs
    _, core = chip_and_core()
    copies = []
    for at, source in enumerate(sources):
        begin, end = cuts(out.shape[2])[at % CHUNKS]
        height = end - begin
        for chip in range(out.shape[0]):
            target = out.at[chip, core if at < CHUNKS else 1 - core, pl.ds(begin, height)]
            copies.append(pltpu.make_async_copy(source.at[pl.ds(chip * height, height)], target, sems.at[at, chip]))
    for copy in copies:
        copy.start()
    token[...] = jnp.zeros_like(token)
    for copy in copies:
        copy.wait()


def subtract(cols, *refs):
    *shares, out = refs
    total = shares[0][...]
    for share in shares[1:]:
        total = total + share[...]
    out[...] = cols[...] - total


def between_chips(value, pairs):
    pairs = [(2 * a + core, 2 * b + core) for a, b in pairs for core in (0, 1)]
    return lax.ppermute(value, "panel", pairs)


def to_other_core(value):
    return lax.ppermute(value, "panel", [(q, q ^ 1) for q in range(lax.axis_size("panel"))])


def gather_rows(value, order):
    count = lax.axis_size("row")
    moved = [lax.ppermute(value, "row", [(j, (j + s) % count) for j in range(count)]) for s in order if s]
    return [value, *moved]


def on_device(slab, boundary, diag_inverse, sub_block, tail_coupling, tail_cols):
    panels, count = lax.axis_size("panel"), lax.axis_size("row")
    chips = panels // 2
    chip, core = chip_and_core()
    rows, width = slab.shape
    piece = rows // panels
    held = chips * piece

    def blocks(array):
        return array.reshape(chips, 2, piece, width)

    own = gather_rows(jnp.concatenate([diag_inverse, sub_block]), weight_shifts(count))
    across_slab = to_other_core(slab)
    other = [to_other_core(shard) for shard in own]
    square = (width, width)
    part = (held, width)
    slices = [(chips * (end - begin), width) for begin, end in cuts(piece)]
    three = (chips, piece, width)
    kept, entering, coupling = call(
        fetch,
        [three, three, tail_coupling.shape],
        [blocks(slab), blocks(boundary), tail_coupling],
        [pltpu.SemaphoreType.DMA((3,))],
        hbm=3,
    )
    map_a, both, coupling, *made = call(
        functools.partial(prepare, count),
        [square, square, tail_coupling.shape] + slices * 2,
        [*own, *other, blocks(across_slab), kept, entering, coupling],
        [pltpu.VMEM((2, *square), jnp.float32)] * 2 + [pltpu.VMEM(part, jnp.float32)],
    )
    parts, carries = made[:CHUNKS], made[CHUNKS:]

    def spread(after):
        near, pieces = 1, [coupling]
        while near < count:
            if len(pieces) > 1:
                pieces = call(packed, [(near * coupling.shape[0], width)], pieces)
            pieces = [pieces[0], lax.ppermute(pieces[0], "row", [(j, j ^ near) for j in range(count)])]
            near *= 2
        return call(functools.partial(stacked, count), [square], pieces, after=after)[0]

    def send_map(value, groups):
        return sum(between_chips(value, group) for group in groups if group)

    own_coupling = None
    priors, across = None, None
    half = 1
    while True:
        last = 2 * half >= chips
        sources = [s for s in range(half - 1, chips - 1, 2 * half)]
        pairs = [[(s, s + 1 + j) for s in sources if s + 1 + j < chips] for j in range(half)]
        maps = [[(s, t) for s, t in group if s >= half] for group in pairs]
        arrived, done = [], []
        for k in range(CHUNKS):
            value = carries[k]
            if priors is not None:
                (value,) = call(inclusive, [slices[k]], [value, priors[k], both], span=SCAN_SPAN, after=done)
                done = [value]
                if k == 0 and half == 2:
                    own_coupling = spread(done)
            arrived.append([between_chips(value, group) for group in reversed(pairs)])
        if last and priors is not None:
            break
        if priors is None:
            priors = [a[0] for a in arrived]
            if any(maps):
                across = send_map(both, maps)
        else:
            (send,) = call(functools.partial(joined, half), [square], [both, across])
            step_map = send_map(send, maps)
            priors = [
                call(
                    functools.partial(advance, half),
                    [slices[k]],
                    [priors[k], across, *arrived[k]],
                )[0]
                for k in range(CHUNKS)
            ]
            (across,) = call(functools.partial(extend, half), [square], [across, step_map])
        if last:
            arrived = [[] for _ in range(CHUNKS)]
            break
        half *= 2

    if own_coupling is None:
        own_coupling = spread([])
    other_coupling = to_other_core(own_coupling)
    arrivals = len(arrived[0])
    stays, leaves = [], []
    for k in range(CHUNKS):
        stay, leave = call(
            functools.partial(finish, half, arrivals),
            [slices[k]] * 2,
            [parts[k], carries[k], map_a, both] + ([across] if arrivals else []) + [priors[k], *arrived[k]],
            [pltpu.VMEM(slices[k], jnp.float32)],
            span=FINISH_SPAN,
            after=stays[-1:],
        )
        stays.append(stay)
        leaves.append(leave)
    shares = call(
        functools.partial(shared, chips),
        [(piece, width)] * chips,
        [*stays, *leaves, own_coupling, other_coupling],
        [pltpu.VMEM(shape, jnp.float32) for shape in slices],
    )
    shares = list(shares)
    for k in reversed(range(1, chips)):
        shares[k] = between_chips(shares[k], [(a, destination(a, k, chips)) for a in range(chips)])
    came = [to_other_core(leave) for leave in leaves]
    factor, token = pl.pallas_call(
        interleave,
        out_shape=[
            jax.ShapeDtypeStruct((chips, 2, piece, width), jnp.float32),
            jax.ShapeDtypeStruct((8, 128), jnp.float32),
        ],
        in_specs=[VMEM] * (2 * CHUNKS),
        out_specs=[HBM, VMEM],
        scratch_shapes=[pltpu.SemaphoreType.DMA((2 * CHUNKS, chips))],
        compiler_params=pltpu.CompilerParams(vmem_limit_bytes=4 << 20),
        cost_estimate=pl.CostEstimate(flops=0, bytes_accessed=16 * held * width, transcendentals=0),
    )(*stays, *came)
    (tail_out,) = call(subtract, [tail_cols.shape], [tail_cols, *shares], after=[token])
    return factor.reshape(rows, width), tail_out


def solution(mesh):
    placed = (
        P("row", "panel"),
        P("row", None),
        P(("panel", "row"), None),
        P(("panel", "row"), None),
        P(("panel", "row"), None),
        P(("row", "panel"), None),
    )
    return jax.shard_map(
        on_device,
        mesh=mesh,
        in_specs=placed,
        out_specs=(P("row", "panel"), P(("row", "panel"), None)),
        check_vma=False,
    )
```

```python
import functools
import math

import jax
import jax.numpy as jnp
from jax import lax
from jax.experimental import pallas as pl
from jax.experimental.pallas import tpu as pltpu
from jax.sharding import PartitionSpec as P

CHUNKS = 2
FIRST = 1 / 2
SCAN_SPAN = 4_000_000_000
FINISH_SPAN = 2_000_000_000
TAIL_SPAN = 8_000_000_000
NT = (((1,), (1,)), ((), ()))
NN = (((1,), (0,)), ((), ()))
VMEM = pl.BlockSpec(memory_space=pltpu.VMEM)
HBM = pl.BlockSpec(memory_space=pltpu.HBM)
ANY = pl.BlockSpec(memory_space=pl.ANY)


def split(x):
    high = x.astype(jnp.bfloat16)
    return high, (x - high.astype(jnp.float32)).astype(jnp.bfloat16)


def dot3(left, right, dims):
    dot = functools.partial(lax.dot_general, dimension_numbers=dims, preferred_element_type=jnp.float32)
    return dot(left[0], right[0]) + (dot(left[0], right[1]) + dot(left[1], right[0]))


def chip_and_core():
    panel = lax.axis_index("panel")
    return lax.div(panel, 2), lax.rem(panel, 2)


def call(kernel, outs, args, scratch=(), span=0, hbm=0, after=()):
    size = sum(a.size * 4 for a in args) + sum(math.prod(o) * 4 for o in outs)
    inputs = len(args)
    args = [*args[: inputs - hbm], *(pltpu.with_memory_space_constraint(a, pltpu.HBM) for a in args[inputs - hbm :])]

    def body(*refs):
        kernel(*refs[:inputs], *refs[inputs + len(after) :])

    return pl.pallas_call(
        body,
        out_shape=[jax.ShapeDtypeStruct(o, jnp.float32) for o in outs],
        in_specs=[VMEM] * (inputs - hbm) + [HBM] * hbm + [ANY] * len(after),
        out_specs=[VMEM] * len(outs),
        scratch_shapes=list(scratch),
        compiler_params=pltpu.CompilerParams(vmem_limit_bytes=40 << 20),
        cost_estimate=pl.CostEstimate(flops=2 * span, bytes_accessed=size, transcendentals=0),
    )(*args, *after)


def weight_shifts(count):
    return [0, *reversed(range(1, count))]


def shard_rows(count, shift, height):
    start = lax.rem(lax.axis_index("row") + count - shift, count) * height
    return pl.ds(pl.multiple_of(start, height), height)


def take(refs, count):
    return [next(refs) for _ in range(count)]


def cuts(piece):
    unit = 16 if piece % 16 == 0 and piece > 16 else 8
    first = max(unit, int(piece * FIRST) // unit * unit)
    if piece % unit or first >= piece:
        first = piece // 2
    return [(0, first), (first, piece)]


def chunked(ref, *index):
    return jnp.concatenate(
        [ref[(chip, *index, slice(*cut))] for cut in cuts(ref.shape[-2]) for chip in range(ref.shape[0])]
    )


def fetch(slab, bound, coupling, kept, entering, coupling_out, sems):
    _, core = chip_and_core()
    copies = [
        pltpu.make_async_copy(source, target, sems.at[k])
        for k, (source, target) in enumerate(
            ((slab.at[:, core], kept), (bound.at[:, core], entering), (coupling, coupling_out))
        )
    ]
    for copy in copies:
        copy.start()
    for copy in copies:
        copy.wait()


def prepare(count, *refs):
    refs = iter(refs)
    own, other = take(refs, count), take(refs, count)
    given, kept, entering, coupling = take(refs, 4)
    map_ref, both_ref, coupling_out = take(refs, 3)
    part_refs, carry_refs = take(refs, CHUNKS), take(refs, CHUNKS)
    inverse, beneath, part = take(refs, 3)
    chip, core = chip_and_core()
    coupling_out[...] = coupling[...]
    height = own[0].shape[0] // 2
    for at, shift in enumerate(weight_shifts(count)):
        rows = shard_rows(count, shift, height)
        for slot, shards in ((core, own), (1 - core, other)):
            inverse[slot, rows, :] = shards[at][:height, :]
            beneath[slot, rows, :] = shards[at][height:, :]
    inverse_a, inverse_b = split(inverse[0]), split(inverse[1])
    map_ref[...] = dot3(inverse_a, split(beneath[0]), NN)
    map_a = split(map_ref[...])
    map_b = split(dot3(inverse_b, split(beneath[1]), NN))
    both_ref[...] = dot3(map_b, map_a, NN)
    first = core == 0
    got, keep = chunked(given, core), chunked(kept)
    part[...] = dot3(split(jnp.where(first, keep, got)), inverse_a, NT)

    @pl.when(chip == 0)
    def _():
        part[...] -= dot3(split(chunked(entering)), map_a, NT)

    carry = dot3(split(jnp.where(first, got, keep)), inverse_b, NT)
    carry -= dot3(split(part[...]), map_b, NT)
    start = 0
    for k in range(CHUNKS):
        end = start + part_refs[k].shape[0]
        part_refs[k][...] = part[start:end, :]
        carry_refs[k][...] = carry[start:end]
        start = end


def inclusive(carry, prior, both, out):
    out[...] = carry[...] + dot3(split(prior[...]), split(both[...]), NT)


def total(refs):
    value = refs[0][...]
    for more in refs[1:]:
        value = value + more[...]
    return value


def absorb(half, prior, across, arrived, put):
    chip, _ = chip_and_core()
    inner = lax.rem(chip, half) != 0

    @pl.when(inner)
    def _():
        put(prior[...] + dot3(split(total(arrived)), split(across[...]), NT))

    @pl.when(jnp.logical_not(inner))
    def _():
        put(prior[...] + total(arrived))


def advance(half, prior, across, *refs):
    *arrived, out = refs

    def put(value):
        out[...] = value

    absorb(half, prior, across, arrived, put)


def extend(half, across, arrived, out):
    chip, _ = chip_and_core()
    inner = lax.rem(chip, half) != 0
    upper = lax.rem(chip, 2 * half) >= half
    out[...] = across[...]

    @pl.when(jnp.logical_and(upper, inner))
    def _():
        out[...] = dot3(split(across[...]), split(arrived[...]), NN)

    @pl.when(jnp.logical_and(upper, jnp.logical_not(inner)))
    def _():
        out[...] = arrived[...]


def joined(half, both, across, out):
    chip, _ = chip_and_core()
    out[...] = both[...]

    @pl.when(lax.rem(chip, half) != 0)
    def _():
        out[...] = dot3(split(both[...]), split(across[...]), NN)


def finish(half, arrivals, *refs):
    refs = iter(refs)
    part, carry, map_ref, both = take(refs, 4)
    across = next(refs) if arrivals else None
    prior = next(refs)
    arrived = take(refs, arrivals)
    stay, leave, entering = take(refs, 3)
    _, core = chip_and_core()
    first = core == 0

    def put(value):
        entering[...] = value

    if arrivals:
        absorb(half, prior, across, arrived, put)
    else:
        put(prior[...])
    incoming = split(entering[...])
    solved_a = part[...] - dot3(incoming, split(map_ref[...]), NT)
    solved_b = carry[...] + dot3(incoming, split(both[...]), NT)
    stay[...] = jnp.where(first, solved_a, solved_b)
    leave[...] = jnp.where(first, solved_b, solved_a)


def shared(chips, stay, leave, own, other, *refs):
    *outs, tail = refs
    chip, _ = chip_and_core()
    tail[...] = dot3(split(stay[...]), split(own[...]), NN) + dot3(split(leave[...]), split(other[...]), NN)
    height = outs[0].shape[0]
    for shift in range(chips):
        start = pl.multiple_of(destination(chip, shift, chips) * height, height)
        outs[shift][...] = tail[pl.ds(start, height), :]


def destination(chip, shift, chips):
    return chip ^ shift if chips & (chips - 1) == 0 else (chip + shift) % chips


def packed(*refs):
    *sources, out = refs
    at = 0
    for source in sources:
        out[at : at + source.shape[0], :] = source[...]
        at += source.shape[0]


def stacked(count, *refs):
    *sources, out = refs
    row = lax.axis_index("row")
    height = out.shape[0] // count
    at = 0
    for source in sources:
        for k in range(source.shape[0] // height):
            start = pl.multiple_of((row ^ at) * height, height)
            out[pl.ds(start, height), :] = source[k * height : (k + 1) * height, :]
            at += 1


def interleave(*refs):
    *sources, out, token, sems = refs
    _, core = chip_and_core()
    copies = []
    for at, source in enumerate(sources):
        begin, end = cuts(out.shape[2])[at % CHUNKS]
        height = end - begin
        for chip in range(out.shape[0]):
            target = out.at[chip, core if at < CHUNKS else 1 - core, pl.ds(begin, height)]
            copies.append(pltpu.make_async_copy(source.at[pl.ds(chip * height, height)], target, sems.at[at, chip]))
    for copy in copies:
        copy.start()
    token[...] = jnp.zeros_like(token)
    for copy in copies:
        copy.wait()


def subtract(chips, cols, *refs):
    *shares, out = refs
    for k, (begin, end) in enumerate(cuts(out.shape[0])):
        out[begin:end, :] = cols[begin:end, :] - total(shares[k * chips : (k + 1) * chips])


def between_chips(value, pairs):
    pairs = [(2 * a + core, 2 * b + core) for a, b in pairs for core in (0, 1)]
    return lax.ppermute(value, "panel", pairs)


def to_other_core(value):
    return lax.ppermute(value, "panel", [(q, q ^ 1) for q in range(lax.axis_size("panel"))])


def gather_rows(value, order):
    count = lax.axis_size("row")
    moved = [lax.ppermute(value, "row", [(j, (j + s) % count) for j in range(count)]) for s in order if s]
    return [value, *moved]


def on_device(slab, boundary, diag_inverse, sub_block, tail_coupling, tail_cols):
    panels, count = lax.axis_size("panel"), lax.axis_size("row")
    chips = panels // 2
    chip, core = chip_and_core()
    rows, width = slab.shape
    piece = rows // panels
    held = chips * piece

    def blocks(array):
        return array.reshape(chips, 2, piece, width)

    own = gather_rows(jnp.concatenate([diag_inverse, sub_block]), weight_shifts(count))
    across_slab = to_other_core(slab)
    other = [to_other_core(shard) for shard in own]
    square = (width, width)
    part = (held, width)
    slices = [(chips * (end - begin), width) for begin, end in cuts(piece)]
    three = (chips, piece, width)
    kept, entering, coupling = call(
        fetch,
        [three, three, tail_coupling.shape],
        [blocks(slab), blocks(boundary), tail_coupling],
        [pltpu.SemaphoreType.DMA((3,))],
        hbm=3,
    )
    map_a, both, coupling, *made = call(
        functools.partial(prepare, count),
        [square, square, tail_coupling.shape] + slices * 2,
        [*own, *other, blocks(across_slab), kept, entering, coupling],
        [pltpu.VMEM((2, *square), jnp.float32)] * 2 + [pltpu.VMEM(part, jnp.float32)],
    )
    parts, carries = made[:CHUNKS], made[CHUNKS:]

    def spread(after):
        near, pieces = 1, [coupling]
        while near < count:
            if len(pieces) > 1:
                pieces = call(packed, [(near * coupling.shape[0], width)], pieces)
            pieces = [pieces[0], lax.ppermute(pieces[0], "row", [(j, j ^ near) for j in range(count)])]
            near *= 2
        return call(functools.partial(stacked, count), [square], pieces, after=after)[0]

    def send_map(value, groups):
        return sum(between_chips(value, group) for group in groups if group)

    own_coupling = None
    priors, across = None, None
    half = 1
    while True:
        last = 2 * half >= chips
        sources = [s for s in range(half - 1, chips - 1, 2 * half)]
        pairs = [[(s, s + 1 + j) for s in sources if s + 1 + j < chips] for j in range(half)]
        maps = [[(s, t) for s, t in group if s >= half] for group in pairs]
        arrived, done = [], []
        for k in range(CHUNKS):
            value = carries[k]
            if priors is not None:
                (value,) = call(inclusive, [slices[k]], [value, priors[k], both], span=SCAN_SPAN, after=done)
                done = [value]
                if k == 0 and half == 2:
                    own_coupling = spread(done)
            arrived.append([between_chips(value, group) for group in reversed(pairs)])
        if last and priors is not None:
            break
        if priors is None:
            priors = [a[0] for a in arrived]
            if any(maps):
                across = send_map(both, maps)
        else:
            (send,) = call(functools.partial(joined, half), [square], [both, across])
            step_map = send_map(send, maps)
            priors = [
                call(
                    functools.partial(advance, half),
                    [slices[k]],
                    [priors[k], across, *arrived[k]],
                )[0]
                for k in range(CHUNKS)
            ]
            (across,) = call(functools.partial(extend, half), [square], [across, step_map])
        if last:
            arrived = [[] for _ in range(CHUNKS)]
            break
        half *= 2

    if own_coupling is None:
        own_coupling = spread([])
    other_coupling = to_other_core(own_coupling)
    arrivals = len(arrived[0])
    stays, leaves, shares = [], [], []
    for k in range(CHUNKS):
        stay, leave = call(
            functools.partial(finish, half, arrivals),
            [slices[k]] * 2,
            [parts[k], carries[k], map_a, both] + ([across] if arrivals else []) + [priors[k], *arrived[k]],
            [pltpu.VMEM(slices[k], jnp.float32)],
            span=FINISH_SPAN,
            after=shares[-1:],
        )
        stays.append(stay)
        leaves.append(leave)
        begin, end = cuts(piece)[k]
        own_share, *others = call(
            functools.partial(shared, chips),
            [(end - begin, width)] * chips,
            [stay, leave, own_coupling, other_coupling],
            [pltpu.VMEM(slices[k], jnp.float32)],
            span=TAIL_SPAN,
        )
        for j in reversed(range(1, chips)):
            others[j - 1] = between_chips(others[j - 1], [(a, destination(a, j, chips)) for a in range(chips)])
        shares += [*others, own_share]
    came = [to_other_core(leave) for leave in leaves]
    factor, token = pl.pallas_call(
        interleave,
        out_shape=[
            jax.ShapeDtypeStruct((chips, 2, piece, width), jnp.float32),
            jax.ShapeDtypeStruct((8, 128), jnp.float32),
        ],
        in_specs=[VMEM] * (2 * CHUNKS),
        out_specs=[HBM, VMEM],
        scratch_shapes=[pltpu.SemaphoreType.DMA((2 * CHUNKS, chips))],
        compiler_params=pltpu.CompilerParams(vmem_limit_bytes=4 << 20),
        cost_estimate=pl.CostEstimate(flops=0, bytes_accessed=16 * held * width, transcendentals=0),
    )(*stays, *came)
    (tail_out,) = call(functools.partial(subtract, chips), [tail_cols.shape], [tail_cols, *shares], after=[token])
    return factor.reshape(rows, width), tail_out


def solution(mesh):
    placed = (
        P("row", "panel"),
        P("row", None),
        P(("panel", "row"), None),
        P(("panel", "row"), None),
        P(("panel", "row"), None),
        P(("row", "panel"), None),
    )
    return jax.shard_map(
        on_device,
        mesh=mesh,
        in_specs=placed,
        out_specs=(P("row", "panel"), P(("row", "panel"), None)),
        check_vma=False,
    )
```
